32 devices in a mesh: gx: 4 (over x, core), gy: 8 (over z, y).
Axes of the slice: x: 2, y: 2, z: 4, core: 2. Of those that a mesh axis runs over, the one named last changes fastest.
Arguments:
- hidden: bfloat16 [256, 16384], P('gy'), may hold values from -6 to 6
- norm_gain: bfloat16 [16384], replicated, may hold values from 0.099609375 to 1.8984375
- w_query: bfloat16 [16384, 16384], P('gx', 'gy'), may hold values from -0.046875 to 0.046875
- w_keyval: bfloat16 [16384, 2048], P('gx', 'gy'), may hold values from -0.046875 to 0.046875
- key_cache: bfloat16 [256, 256, 8, 128], P(('gx', 'gy')), may hold values from -1000 to 1000
- value_cache: bfloat16 [256, 256, 8, 128], P(('gx', 'gy')), may hold values from -16 to 16
- lengths: int32 [256], P(('gx', 'gy')), may hold values from 1 to 256, as said below
- w_out: bfloat16 [16384, 16384], P('gy', 'gx'), may hold values from -0.046875 to 0.046875
Outputs:
- mixed: bfloat16 [256, 16384], P('gy', 'gx')
The draws below stay inside these ranges and needn't reach their ends.
Inputs may be any that keep to these rules, and one draw needn't show every extreme that they name: Slots 0 to lengths - 1 of a row are filled; some row fills all 256.
All inputs are finite; a program needn't handle non-finite values.
Results may differ from the reference program's by a relative error of at most 0.024.
Values may be sent and summed in bfloat16 or wider, within the bound.
A program may use at most 128 MiB of HBM per device.

```python
import math
import jax
import jax.numpy as jnp
from jax import lax

D = 16384
HEADS = 128
KV_HEADS = 8
HEAD_DIM = 128
CACHE = 256
ROWS = 256


def draw_key_cache(key, part):
    base_key = jax.random.fold_in(jax.random.fold_in(key, 11), 0)
    shape = (ROWS, CACHE, KV_HEADS, HEAD_DIM)
    base = jnp.clip(jax.random.normal(base_key, shape, jnp.float32), -6.0, 6.0)
    return base.astype(jnp.bfloat16)


def draw_lengths(key, part):
    drawn = jax.random.randint(jax.random.fold_in(key, 23), (ROWS,), 1, CACHE + 1, dtype=jnp.int32)
    return drawn.at[0].set(CACHE)


def block_levels(stream_key, shape, cuts, low, high):
    def one(dim, parts):
        steps = jax.random.uniform(jax.random.fold_in(jax.random.fold_in(stream_key, 6), dim), (parts,), jnp.float32, low / len(cuts), high / len(cuts))
        return jnp.repeat(jnp.exp(steps), shape[dim] // parts).reshape((-1,) + (1,) * (len(shape) - dim - 1))

    factor_of = one(*cuts[0])
    for cut in cuts[1:]:
        factor_of = factor_of * one(*cut)
    return factor_of


def normal_values(stream_key, dims, width, most, cuts=(), kind=jnp.bfloat16):
    values = width * jax.random.normal(stream_key, dims, jnp.float32)
    if cuts:
        values = values * block_levels(stream_key, dims, cuts, -0.22, 0.18)
    return jnp.clip(values, -most, most).astype(kind)


def setup_inputs(seed: int = 0) -> dict:
    key_list = jax.random.split(jax.random.key(seed), 9)
    hidden = normal_values(key_list[0], (ROWS, D), 1.0, 6.0, ((0, 8),))
    norm_gain = jnp.clip(1.0 + 0.18 * jax.random.normal(key_list[1], (D,), jnp.float32), 0.099609375, 1.8984375).astype(jnp.bfloat16)
    w_query = normal_values(key_list[2], (D, HEADS * HEAD_DIM), D ** -0.5, 0.046875, ((0, 4), (1, 8)))
    w_keyval = normal_values(key_list[3], (D, 2 * KV_HEADS * HEAD_DIM), D ** -0.5, 0.046875, ((0, 4), (1, 8)))
    key_cache = draw_key_cache(jax.random.fold_in(key_list[8], 71), 0)
    value_cache = normal_values(key_list[5], (ROWS, CACHE, KV_HEADS, HEAD_DIM), 4.0, 16.0, ((0, 32),))
    lengths = draw_lengths(jax.random.fold_in(key_list[8], 71), 0)
    w_out = normal_values(key_list[7], (HEADS * HEAD_DIM, D), (HEADS * HEAD_DIM) ** -0.5, 0.046875, ((0, 8), (1, 4)))
    return {"hidden": hidden, "norm_gain": norm_gain, "w_query": w_query, "w_keyval": w_keyval, "key_cache": key_cache, "value_cache": value_cache, "lengths": lengths, "w_out": w_out}


def rotate_heads(values, position, head_dim):
    half = head_dim // 2
    freq = jnp.exp(-(jnp.arange(half, dtype=jnp.float32) * 2.0 / head_dim) * math.log(500000.0))
    angle = position[:, None] * freq[None, :]
    cosine = jnp.cos(angle)[:, None, :]
    sine = jnp.sin(angle)[:, None, :]
    first = values[..., :half]
    second = values[..., half:]
    return jnp.concatenate([first * cosine - second * sine, second * cosine + first * sine], axis=-1)

def attend_block(query, keyval, key_block, value_block, length_block):
    rows, cache_len, kv_heads, head_dim = key_block.shape
    heads = query.shape[1] // head_dim
    group = heads // kv_heads
    scale = 1.0 / math.sqrt(head_dim)
    position = length_block.astype(jnp.float32)
    rotated = rotate_heads(query.astype(jnp.float32).reshape(rows, heads, head_dim), position, head_dim).astype(jnp.bfloat16)
    pairs = keyval.reshape(rows, 2, kv_heads, head_dim)
    new_key = rotate_heads(pairs[:, 0].astype(jnp.float32), position, head_dim).astype(jnp.bfloat16)
    new_value = pairs[:, 1].astype(jnp.float32)
    grouped = rotated.astype(jnp.float32).reshape(rows, kv_heads, group, head_dim)
    scores = jnp.einsum('rgqd,rtgd->rgqt', grouped, key_block.astype(jnp.float32)) * scale
    own = jnp.einsum('rgqd,rgd->rgq', grouped, new_key.astype(jnp.float32)) * scale
    valid = jnp.arange(cache_len)[None, None, None, :] < length_block[:, None, None, None]
    scores = jnp.where(valid, scores, -jnp.inf)
    top = jnp.maximum(lax.optimization_barrier(jnp.max(scores, axis=-1)), own)
    weights = jnp.exp(scores - top[..., None])
    own_weight = jnp.exp(own - top)
    total = lax.optimization_barrier(jnp.sum(weights, axis=-1)) + own_weight
    probs = (weights / total[..., None]).astype(jnp.bfloat16)
    own_prob = (own_weight / total).astype(jnp.bfloat16)
    result = jnp.einsum('rgqt,rtgd->rgqd', probs.astype(jnp.float32), value_block.astype(jnp.float32))
    result = result + own_prob.astype(jnp.float32)[..., None] * new_value[:, :, None, :]
    return result.astype(jnp.bfloat16).reshape(rows, heads * head_dim)

def reference(hidden, norm_gain, w_query, w_keyval, key_cache, value_cache, lengths, w_out):
    values = hidden.astype(jnp.float32)
    inverse = lax.rsqrt(lax.optimization_barrier(jnp.mean(values * values, axis=1, keepdims=True)) + 1e-05)
    normed = (values * inverse * norm_gain.astype(jnp.float32)).astype(jnp.bfloat16)
    query = jnp.dot(normed, w_query, preferred_element_type=jnp.float32).astype(jnp.bfloat16)
    keyval = jnp.dot(normed, w_keyval, preferred_element_type=jnp.float32).astype(jnp.bfloat16)
    block = 8
    count = ROWS // block

    def one_block(items):
        return attend_block(*items)
    attended = lax.map(one_block, (query.reshape(count, block, query.shape[1]), keyval.reshape(count, block, keyval.shape[1]), key_cache.reshape((count, block) + key_cache.shape[1:]), value_cache.reshape((count, block) + value_cache.shape[1:]), lengths.reshape(count, block)))
    attended = attended.reshape(ROWS, HEADS * HEAD_DIM)
    return jnp.dot(attended, w_out, preferred_element_type=jnp.float32).astype(jnp.bfloat16)
```

```python
import functools
import math

import jax
import jax.numpy as jnp
from jax import lax
from jax.experimental import pallas as pl
from jax.experimental.pallas import tpu as pltpu
from jax.sharding import PartitionSpec as P

MESH = pl.DeviceIdType.MESH
VMEM_BYTES = 56 * 2**20


def rotate_heads(values, position, head_dim):
    half = head_dim // 2
    freq = jnp.exp(-(jnp.arange(half, dtype=jnp.float32) * 2.0 / head_dim) * math.log(500000.0))
    angle = position[:, None] * freq[None, :]
    cosine = jnp.cos(angle)[:, None, :]
    sine = jnp.sin(angle)[:, None, :]
    first = values[..., :half]
    second = values[..., half:]
    return jnp.concatenate(
        [first * cosine - second * sine, second * cosine + first * sine], axis=-1
    )


def attend_rows(query, keyval, key_cache, value_cache, lengths):
    rows, cache_len, kv_heads, head_dim = key_cache.shape
    heads = query.shape[1] // head_dim
    group = heads // kv_heads
    scale = 1.0 / math.sqrt(head_dim)
    position = lengths.astype(jnp.float32)
    rotated = rotate_heads(
        query.astype(jnp.float32).reshape(rows, heads, head_dim), position, head_dim
    ).astype(jnp.bfloat16)
    pairs = keyval.reshape(rows, 2, kv_heads, head_dim)
    new_key = rotate_heads(pairs[:, 0].astype(jnp.float32), position, head_dim).astype(jnp.bfloat16)
    new_value = pairs[:, 1].astype(jnp.float32)
    grouped = rotated.reshape(rows, kv_heads, group, head_dim)
    scores = (
        jnp.einsum("rgqd,rtgd->rgqt", grouped, key_cache, preferred_element_type=jnp.float32)
        * scale
    )
    own = jnp.einsum("rgqd,rgd->rgq", grouped, new_key, preferred_element_type=jnp.float32) * scale
    valid = jnp.arange(cache_len)[None, None, None, :] < lengths[:, None, None, None]
    scores = jnp.where(valid, scores, -jnp.inf)
    top = jnp.maximum(jnp.max(scores, axis=-1), own)
    weights = jnp.exp(scores - top[..., None])
    own_weight = jnp.exp(own - top)
    total = jnp.sum(weights, axis=-1) + own_weight
    probs = (weights / total[..., None]).astype(jnp.bfloat16)
    own_prob = (own_weight / total).astype(jnp.bfloat16)
    result = jnp.einsum("rgqt,rtgd->rgqd", probs, value_cache, preferred_element_type=jnp.float32)
    result = result + own_prob.astype(jnp.float32)[..., None] * new_value[:, :, None, :]
    return result.astype(jnp.bfloat16).reshape(rows, heads * head_dim)


def position_of(index, n):
    return jnp.where(lax.rem(index, 2) == 0, index // 2, n - (index + 1) // 2)


def index_at(position, n):
    position = lax.rem(position + 2 * n, n)
    return jnp.where(position < n // 2, 2 * position, 2 * n - 2 * position - 1)


def meet(n, gx, me):
    barrier = pltpu.get_barrier_semaphore()
    for k in range(1, n):
        pl.semaphore_signal(
            barrier, inc=1, device_id=(gx, lax.rem(me + k, n)), device_id_type=MESH
        )
    pl.semaphore_signal(barrier, inc=1, device_id=(sibling(gx), me), device_id_type=MESH)
    pl.semaphore_signal(barrier, inc=1, device_id=(across(gx), me), device_id_type=MESH)
    pl.semaphore_wait(barrier, n + 1)


def sibling(gx):
    return gx + 1 - 2 * lax.rem(gx, 2)


def across(gx):
    return lax.rem(gx + 2, 4)


def send(src, dst, send_sem, recv_sem, device):
    copy = pltpu.make_async_remote_copy(
        src_ref=src,
        dst_ref=dst,
        send_sem=send_sem,
        recv_sem=recv_sem,
        device_id=device,
        device_id_type=MESH,
    )
    return copy


def halves_stacked(block):
    half = block.shape[1] // 2
    return jnp.concatenate([block[:, :half], block[:, half:]], axis=0)


def project_kernel(
    n, chunks, tiles,
    hidden_ref, gain_ref, wq_hbm, wkv_hbm, q_out, kv_out,
    wq, wkv, xg, *rest,
):
    count = len(tiles)
    acc = rest[:count]
    s1, r1, s2, r2, s3, r3 = (rest[count * (k + 1) : count * (k + 2)] for k in range(6))
    (w_sem, ag_send, ag_recv, s1_send, s1_recv, s2_send, s2_recv, s3_send, s3_recv) = rest[
        count * 7 :
    ]
    gx = lax.axis_index("gx")
    me = lax.axis_index("gy")
    rows = hidden_ref.shape[0]
    total = rows * n
    width = chunks * xg.shape[2]
    piece = xg.shape[2]
    hops = n // 2
    loads = []
    for c in range(chunks):
        loads.append(
            (
                pltpu.make_async_copy(
                    wq_hbm.at[pl.ds(c * piece, piece), :], wq.at[c], w_sem.at[0, c]
                ),
                pltpu.make_async_copy(
                    wkv_hbm.at[pl.ds(c * piece, piece), :], wkv.at[c], w_sem.at[1, c]
                ),
            )
        )
    for pair in loads:
        pair[0].start()
        pair[1].start()

    squares = jnp.zeros((rows, 128), jnp.float32)
    features = hidden_ref.shape[1]
    for k in range(0, features, 1024):
        block = hidden_ref[:, k : k + 1024].astype(jnp.float32)
        block = block * block
        for part in range(0, 1024, 128):
            squares = squares + block[:, part : part + 128]
    mean = jnp.sum(squares, axis=1, keepdims=True) * (1.0 / features)
    inverse = lax.rsqrt(mean + 1e-05)

    place = position_of(me, n)
    ahead = index_at(place + 1, n)
    behind = index_at(place - 1, n)
    targets = (ahead, behind)

    def slot(owner, c):
        return xg.at[c, pl.ds(pl.multiple_of(owner * rows, rows), rows), :]

    def used(d, c, s):
        return s < hops - 1 or c % 2 == d

    def ring(d, c, s):
        owner = index_at(place - s if d == 0 else place + s, n)
        ref = slot(owner, c)
        return send(ref, ref, ag_send.at[d, c, s], ag_recv.at[d, c, s], (gx, targets[d]))

    def ring_in(d, c, s):
        owner = index_at(place - s - 1 if d == 0 else place + s + 1, n)
        ref = slot(owner, c)
        return send(ref, ref, ag_send.at[d, c, s], ag_recv.at[d, c, s], (gx, targets[d]))

    for c in range(chunks):
        offset = pl.multiple_of(gx * width + c * piece, piece)
        block = hidden_ref[:, pl.ds(offset, piece)].astype(jnp.float32)
        gain = gain_ref[:, pl.ds(offset, piece)].astype(jnp.float32)
        xg[c, pl.ds(pl.multiple_of(me * rows, rows), rows), :] = (
            block * inverse * gain
        ).astype(jnp.bfloat16)
    meet(n, gx, me)

    started = []

    def go(copy):
        copy.start()
        started.append(copy)

    def add_product(t, c):
        source, start, wide = tiles[t]
        weights = wq if source == 0 else wkv
        step = min(512, wide)

        def body(k, carry):
            at = pl.multiple_of(k * step, step) if wide > step else 0
            product = jnp.dot(
                xg[c],
                weights[c, :, pl.ds(start + at, step)],
                preferred_element_type=jnp.float32,
            )
            if c == 0:
                acc[t][:, pl.ds(at, step)] = product
            else:
                acc[t][:, pl.ds(at, step)] += product
            return carry

        if wide > step:
            lax.fori_loop(0, wide // step, body, 0)
        else:
            body(0, 0)

    part_rows = total // 4
    core = lax.rem(gx, 2)
    xi = gx // 2

    def part(gxi):
        return pl.ds(pl.multiple_of(gxi * part_rows, part_rows), part_rows)

    first = []
    for time in range(chunks + hops):
        if time == 0:
            for c in range(min(2, chunks)):
                for d in (0, 1):
                    if used(d, c, 0):
                        go(ring(d, c, 0))
        elif time + 1 < chunks:
            for d in (0, 1):
                if used(d, time + 1, 0):
                    go(ring(d, time + 1, 0))
        for c in range(chunks):
            s = time - c
            if 1 <= s < hops:
                for d in (0, 1):
                    if used(d, c, s - 1):
                        ring_in(d, c, s - 1).wait_recv()
                    if used(d, c, s):
                        go(ring(d, c, s))
        c = time - hops
        if 0 <= c < chunks:
            for d in (0, 1):
                if used(d, c, hops - 1):
                    ring_in(d, c, hops - 1).wait_recv()
            loads[c][0].wait()
            loads[c][1].wait()
            for t in range(count):
                add_product(t, c)
                if c == chunks - 1:
                    for x in (0, 1):
                        s1[t][x] = acc[t][part(2 * x + 1 - core), :].astype(jnp.bfloat16)
                    copy = send(s1[t], r1[t], s1_send.at[t], s1_recv.at[t], (sibling(gx), me))
                    go(copy)
                    first.append(copy)
    second = []
    for t in range(count):
        first[t].wait_recv()
        s2[t][...] = (
            acc[t][part(across(gx)), :] + r1[t][1 - xi].astype(jnp.float32)
        ).astype(jnp.bfloat16)
        copy = send(s2[t], r2[t], s2_send.at[t], s2_recv.at[t], (across(gx), me))
        go(copy)
        second.append(copy)
    for t in range(count):
        second[t].wait_recv()
        block = acc[t][part(gx), :] + r1[t][xi].astype(jnp.float32) + r2[t][...].astype(jnp.float32)
        for p in range(n):
            s3[t][p] = halves_stacked(block[8 * p : 8 * p + 8, :]).astype(jnp.bfloat16)
        for k in range(1, n):
            go(
                send(
                    s3[t].at[lax.rem(me + k, n)],
                    r3[t].at[me],
                    s3_send.at[t, k],
                    s3_recv.at[t, k],
                    (gx, lax.rem(me + k, n)),
                )
            )
        r3[t][me] = s3[t][me]
    for t in range(count):
        for k in range(1, n):
            owner = lax.rem(me + n - k, n)
            send(
                s3[t].at[owner], r3[t].at[owner], s3_send.at[t, k], s3_recv.at[t, k], (gx, owner)
            ).wait_recv()
        source, start, wide = tiles[t]
        out = q_out if source == 0 else kv_out
        columns = out.shape[1] // n
        half = wide // 2
        for p in range(n):
            block = r3[t][p].astype(jnp.float32)
            at = p * columns + start
            out[:, at : at + half] = block[:8].astype(jnp.bfloat16)
            out[:, at + half : at + wide] = block[8:].astype(jnp.bfloat16)
    for copy in started:
        copy.wait_send()


def project(hidden, gain, w_query, w_keyval, n):
    rows, features = hidden.shape
    width, q_cols = w_query.shape
    kv_cols = w_keyval.shape[1]
    chunks = 4
    piece = width // chunks
    total = rows * n
    step = min(1024, q_cols)
    tiles = [(0, k, step) for k in range(0, q_cols, step)] + [(1, 0, kv_cols)]
    count = len(tiles)
    hops = n // 2
    bf = jnp.bfloat16
    scratch = [
        pltpu.VMEM((chunks, piece, q_cols), bf),
        pltpu.VMEM((chunks, piece, kv_cols), bf),
        pltpu.VMEM((chunks, total, piece), bf),
    ]
    scratch += [pltpu.VMEM((total, w), jnp.float32) for _, _, w in tiles]
    for shape in (
        lambda w: (2, total // 4, w),
        lambda w: (2, total // 4, w),
        lambda w: (total // 4, w),
        lambda w: (total // 4, w),
        lambda w: (n, 16, w // 2),
        lambda w: (n, 16, w // 2),
    ):
        scratch += [pltpu.VMEM(shape(w), bf) for _, _, w in tiles]
    dma = pltpu.SemaphoreType.DMA
    scratch += [
        dma((2, chunks)),
        dma((2, chunks, hops)), dma((2, chunks, hops)),
        dma((count,)), dma((count,)),
        dma((count,)), dma((count,)),
        dma((count, n)), dma((count, n)),
    ]
    vmem = pl.BlockSpec(memory_space=pltpu.VMEM)
    hbm = pl.BlockSpec(memory_space=pl.ANY)
    return pl.pallas_call(
        functools.partial(project_kernel, n, chunks, tiles),
        out_shape=[
            jax.ShapeDtypeStruct((8, n * q_cols), bf),
            jax.ShapeDtypeStruct((8, n * kv_cols), bf),
        ],
        in_specs=[vmem, vmem, hbm, hbm],
        out_specs=[vmem, vmem],
        scratch_shapes=scratch,
        compiler_params=pltpu.CompilerParams(
            collective_id=0, has_side_effects=True, vmem_limit_bytes=VMEM_BYTES
        ),
        cost_estimate=pl.CostEstimate(
            flops=2 * total * width * (q_cols + kv_cols),
            bytes_accessed=2 * width * (q_cols + kv_cols),
            transcendentals=0,
        ),
        name="project",
    )(hidden, gain, w_query, w_keyval)


def combine_kernel(
    n, chunks,
    att_ref, w_hbm, out_ref,
    w, packed, xa, xs, part, first, ringbuf,
    w_sem, a_send, a_recv, x_send, x_recv, c_send, c_recv, e_send, e_recv, g_send, g_recv,
):
    gx = lax.axis_index("gx")
    me = lax.axis_index("gy")
    columns = w.shape[1]
    piece = w.shape[2]
    half = columns // 2
    hops = n // 2
    total = xs.shape[0]
    rows = total // n
    loads = [
        pltpu.make_async_copy(w_hbm.at[:, pl.ds(c * piece, piece)], w.at[c], w_sem.at[c])
        for c in range(chunks)
    ]
    for p in range(n):
        block = att_ref[:, p * columns : (p + 1) * columns].astype(jnp.float32)
        packed[p] = halves_stacked(block).astype(jnp.bfloat16)
    started = []

    def go(copy):
        copy.start()
        started.append(copy)

    meet(n, gx, me)
    for k in range(1, n):
        to = lax.rem(me + k, n)
        go(send(packed.at[to], xa.at[gx, me], a_send.at[k], a_recv.at[k], (gx, to)))
    for load in loads:
        load.start()
    xa[gx, me] = packed[me]
    other = across(gx)
    twin = sibling(gx)
    far = across(twin)
    for k in range(n):
        owner = lax.rem(me + n - k, n)
        if k:
            send(packed.at[owner], xa.at[gx, owner], a_send.at[k], a_recv.at[k], (gx, owner)).wait_recv()
        ref = xa.at[gx, owner]
        go(send(ref, ref, x_send.at[k], x_recv.at[k], (other, me)))
        go(send(ref, ref, c_send.at[k], c_recv.at[k], (twin, me)))
    for k in range(n):
        owner = lax.rem(me + n - k, n)
        ref = xa.at[other, owner]
        send(ref, ref, x_send.at[k], x_recv.at[k], (other, me)).wait_recv()
        go(send(ref, ref, e_send.at[k], e_recv.at[k], (twin, me)))
    for k in range(n):
        owner = lax.rem(me + n - k, n)
        ref = xa.at[twin, owner]
        send(ref, ref, c_send.at[k], c_recv.at[k], (twin, me)).wait_recv()
    for k in range(n):
        owner = lax.rem(me + n - k, n)
        ref = xa.at[far, owner]
        send(ref, ref, e_send.at[k], e_recv.at[k], (twin, me)).wait_recv()
    for i in range(4):
        for p in range(0, n, 2):
            low = xa[i, p].astype(jnp.float32)
            high = xa[i, p + 1].astype(jnp.float32)
            at = (i * n + p) * 8
            xs[at : at + 16, :half] = jnp.concatenate([low[:8], high[:8]], axis=0).astype(jnp.bfloat16)
            xs[at : at + 16, half:] = jnp.concatenate([low[8:], high[8:]], axis=0).astype(jnp.bfloat16)

    place = position_of(me, n)
    targets = (index_at(place + 1, n), index_at(place - 1, n))

    def used(d, c, s):
        return s > 0 or c % 2 == d

    def own(c, owner):
        return part[c, pl.ds(pl.multiple_of(owner * rows, rows), rows), :]

    def hop(d, c, s):
        begins = not (s > 0 and used(d, c, s - 1))
        src = first.at[d, c] if begins else ringbuf.at[d, c, s - 1]
        return send(src, ringbuf.at[d, c, s], g_send.at[d, c, s], g_recv.at[d, c, s], (gx, targets[d]))

    def pass_on(d, c, s):
        away = hops - s
        owner = index_at(place + away if d == 0 else place - away, n)
        value = own(c, owner)
        if s > 0 and used(d, c, s - 1):
            hop(d, c, s - 1).wait_recv()
            ringbuf[d, c, s - 1] = (
                value + ringbuf[d, c, s - 1].astype(jnp.float32)
            ).astype(jnp.bfloat16)
        else:
            first[d, c] = value.astype(jnp.bfloat16)
        go(hop(d, c, s))

    step = min(512, piece)
    for time in range(chunks + hops):
        for c in range(chunks):
            s = time - c
            if 1 <= s < hops:
                for d in (0, 1):
                    pass_on(d, c, s)
            if s == hops:
                value = own(c, me)
                for d in (0, 1):
                    hop(d, c, hops - 1).wait_recv()
                    value = value + ringbuf[d, c, hops - 1].astype(jnp.float32)
                out_ref[:, c * piece : (c + 1) * piece] = value.astype(jnp.bfloat16)
        if time < chunks:
            c = time
            loads[c].wait()

            def body(k, carry):
                at = pl.multiple_of(k * step, step)
                part[c, :, pl.ds(at, step)] = jnp.dot(
                    xs[...], w[c, :, pl.ds(at, step)], preferred_element_type=jnp.float32
                )
                return carry

            lax.fori_loop(0, piece // step, body, 0)
            for d in (0, 1):
                if used(d, c, 0):
                    pass_on(d, c, 0)
    for copy in started:
        copy.wait_send()


def combine(attended, w_out, n):
    columns, width = w_out.shape
    chunks = 4
    piece = width // chunks
    total = 4 * n * 8
    rows = total // n
    hops = n // 2
    bf = jnp.bfloat16
    dma = pltpu.SemaphoreType.DMA
    vmem = pl.BlockSpec(memory_space=pltpu.VMEM)
    hbm = pl.BlockSpec(memory_space=pl.ANY)
    return pl.pallas_call(
        functools.partial(combine_kernel, n, chunks),
        out_shape=jax.ShapeDtypeStruct((rows, width), bf),
        in_specs=[vmem, hbm],
        out_specs=vmem,
        scratch_shapes=[
            pltpu.VMEM((chunks, columns, piece), bf),
            pltpu.VMEM((n, 16, columns // 2), bf),
            pltpu.VMEM((4, n, 16, columns // 2), bf),
            pltpu.VMEM((total, columns), bf),
            pltpu.VMEM((chunks, total, piece), jnp.float32),
            pltpu.VMEM((2, chunks, rows, piece), bf),
            pltpu.VMEM((2, chunks, hops, rows, piece), bf),
            dma((chunks,)),
            dma((n,)), dma((n,)),
            dma((n,)), dma((n,)),
            dma((n,)), dma((n,)),
            dma((n,)), dma((n,)),
            dma((2, chunks, hops)), dma((2, chunks, hops)),
        ],
        compiler_params=pltpu.CompilerParams(
            collective_id=1, has_side_effects=True, vmem_limit_bytes=VMEM_BYTES
        ),
        cost_estimate=pl.CostEstimate(
            flops=2 * total * columns * width,
            bytes_accessed=2 * columns * width,
            transcendentals=0,
        ),
        name="combine",
    )(attended, w_out)


def shards(hidden, norm_gain, w_query, w_keyval, key_cache, value_cache, lengths, w_out):
    peers = lax.axis_size("gy")
    query, keyval = project(hidden, norm_gain.reshape(1, -1), w_query, w_keyval, peers)
    attended = attend_rows(query, keyval, key_cache, value_cache, lengths)
    return combine(attended, w_out, peers)


def solution(mesh):
    in_specs = (
        P("gy", None),
        P(),
        P("gx", "gy"),
        P("gx", "gy"),
        P(("gx", "gy"), None, None, None),
        P(("gx", "gy"), None, None, None),
        P(("gx", "gy")),
        P("gy", "gx"),
    )
    out_specs = P("gy", "gx")
    return jax.shard_map(shards, mesh=mesh, in_specs=in_specs, out_specs=out_specs, check_vma=False)
```

```python
import functools
import math

import jax
import jax.numpy as jnp
from jax import lax
from jax.experimental import pallas as pl
from jax.experimental.pallas import tpu as pltpu
from jax.sharding import PartitionSpec as P

MESH = pl.DeviceIdType.MESH
VMEM_BYTES = 56 * 2**20
GROUP = 2


def rotate_heads(values, position, head_dim):
    half = head_dim // 2
    freq = jnp.exp(-(jnp.arange(half, dtype=jnp.float32) * 2.0 / head_dim) * math.log(500000.0))
    angle = position[:, None] * freq[None, :]
    cosine = jnp.cos(angle)[:, None, :]
    sine = jnp.sin(angle)[:, None, :]
    first = values[..., :half]
    second = values[..., half:]
    return jnp.concatenate(
        [first * cosine - second * sine, second * cosine + first * sine], axis=-1
    )


def attend_rows(query, keyval, key_cache, value_cache, lengths):
    rows, cache_len, kv_heads, head_dim = key_cache.shape
    heads = query.shape[1] // head_dim
    group = heads // kv_heads
    scale = 1.0 / math.sqrt(head_dim)
    position = lengths.astype(jnp.float32)
    rotated = rotate_heads(
        query.astype(jnp.float32).reshape(rows, heads, head_dim), position, head_dim
    ).astype(jnp.bfloat16)
    pairs = keyval.reshape(rows, 2, kv_heads, head_dim)
    new_key = rotate_heads(pairs[:, 0].astype(jnp.float32), position, head_dim).astype(jnp.bfloat16)
    new_value = pairs[:, 1].astype(jnp.float32)
    grouped = rotated.reshape(rows, kv_heads, group, head_dim)
    scores = (
        jnp.einsum("rgqd,rtgd->rgqt", grouped, key_cache, preferred_element_type=jnp.float32)
        * scale
    )
    own = jnp.einsum("rgqd,rgd->rgq", grouped, new_key, preferred_element_type=jnp.float32) * scale
    valid = jnp.arange(cache_len)[None, None, None, :] < lengths[:, None, None, None]
    scores = jnp.where(valid, scores, -jnp.inf)
    top = jnp.maximum(jnp.max(scores, axis=-1), own)
    weights = jnp.exp(scores - top[..., None])
    own_weight = jnp.exp(own - top)
    total = jnp.sum(weights, axis=-1) + own_weight
    probs = (weights / total[..., None]).astype(jnp.bfloat16)
    own_prob = (own_weight / total).astype(jnp.bfloat16)
    result = jnp.einsum("rgqt,rtgd->rgqd", probs, value_cache, preferred_element_type=jnp.float32)
    result = result + own_prob.astype(jnp.float32)[..., None] * new_value[:, :, None, :]
    return result.astype(jnp.bfloat16).reshape(rows, heads * head_dim)


def position_of(index, n):
    return jnp.where(lax.rem(index, 2) == 0, index // 2, n - (index + 1) // 2)


def index_at(position, n):
    position = lax.rem(position + 2 * n, n)
    return jnp.where(position < n // 2, 2 * position, 2 * n - 2 * position - 1)


def meet(n, gx, me):
    barrier = pltpu.get_barrier_semaphore()
    for k in range(1, n):
        pl.semaphore_signal(
            barrier, inc=1, device_id=(gx, lax.rem(me + k, n)), device_id_type=MESH
        )
    pl.semaphore_signal(barrier, inc=1, device_id=(sibling(gx), me), device_id_type=MESH)
    pl.semaphore_signal(barrier, inc=1, device_id=(across(gx), me), device_id_type=MESH)


def met(n):
    pl.semaphore_wait(pltpu.get_barrier_semaphore(), n + 1)


def sibling(gx):
    return gx + 1 - 2 * lax.rem(gx, 2)


def across(gx):
    return lax.rem(gx + 2, 4)


def send(src, dst, send_sem, recv_sem, device):
    copy = pltpu.make_async_remote_copy(
        src_ref=src,
        dst_ref=dst,
        send_sem=send_sem,
        recv_sem=recv_sem,
        device_id=device,
        device_id_type=MESH,
    )
    return copy


def halves_stacked(block):
    half = block.shape[1] // 2
    return jnp.concatenate([block[:, :half], block[:, half:]], axis=0)


def project_kernel(
    n, chunks, tiles,
    hidden_ref, gain_ref, wq_hbm, wkv_hbm, q_out, kv_out,
    wq, wkv, xg, *rest,
):
    count = len(tiles)
    acc = rest[:count]
    s1, r1, s2, r2, s3, r3 = (rest[count * (k + 1) : count * (k + 2)] for k in range(6))
    (w_sem, ag_send, ag_recv, s1_send, s1_recv, s2_send, s2_recv, s3_send, s3_recv) = rest[
        count * 7 :
    ]
    gx = lax.axis_index("gx")
    me = lax.axis_index("gy")
    rows = hidden_ref.shape[0]
    total = rows * n
    width = chunks * xg.shape[2]
    piece = xg.shape[2]
    hops = n // 2
    meet(n, gx, me)
    loads = []
    for c in range(chunks):
        loads.append(
            (
                pltpu.make_async_copy(
                    wq_hbm.at[pl.ds(c * piece, piece), :], wq.at[c], w_sem.at[0, c]
                ),
                pltpu.make_async_copy(
                    wkv_hbm.at[pl.ds(c * piece, piece), :], wkv.at[c], w_sem.at[1, c]
                ),
            )
        )
    for pair in loads:
        pair[0].start()
        pair[1].start()

    squares = jnp.zeros((rows, 128), jnp.float32)
    features = hidden_ref.shape[1]
    for k in range(0, features, 1024):
        block = hidden_ref[:, k : k + 1024].astype(jnp.float32)
        block = block * block
        for part in range(0, 1024, 128):
            squares = squares + block[:, part : part + 128]
    mean = jnp.sum(squares, axis=1, keepdims=True) * (1.0 / features)
    inverse = lax.rsqrt(mean + 1e-05)

    place = position_of(me, n)
    ahead = index_at(place + 1, n)
    behind = index_at(place - 1, n)
    targets = (ahead, behind)

    def slot(owner, c):
        return xg.at[c, pl.ds(pl.multiple_of(owner * rows, rows), rows), :]

    def used(d, c, s):
        return s < hops - 1 or c % 2 == d

    def ring(d, c, s):
        owner = index_at(place - s if d == 0 else place + s, n)
        ref = slot(owner, c)
        return send(ref, ref, ag_send.at[d, c, s], ag_recv.at[d, c, s], (gx, targets[d]))

    def ring_in(d, c, s):
        owner = index_at(place - s - 1 if d == 0 else place + s + 1, n)
        ref = slot(owner, c)
        return send(ref, ref, ag_send.at[d, c, s], ag_recv.at[d, c, s], (gx, targets[d]))

    for c in range(chunks):
        offset = pl.multiple_of(gx * width + c * piece, piece)
        block = hidden_ref[:, pl.ds(offset, piece)].astype(jnp.float32)
        gain = gain_ref[pl.ds(offset, piece)].astype(jnp.float32).reshape(1, piece)
        xg[c, pl.ds(pl.multiple_of(me * rows, rows), rows), :] = (
            block * inverse * gain
        ).astype(jnp.bfloat16)
    met(n)

    started = []

    def go(copy):
        copy.start()
        started.append(copy)

    def add_product(t, c):
        source, start, wide = tiles[t]
        weights = wq if source == 0 else wkv
        step = min(512, wide)

        def body(k, carry):
            at = pl.multiple_of(k * step, step) if wide > step else 0
            product = jnp.dot(
                xg[c],
                weights[c, :, pl.ds(start + at, step)],
                preferred_element_type=jnp.float32,
            )
            if c == 0:
                acc[t][:, pl.ds(at, step)] = product
            else:
                acc[t][:, pl.ds(at, step)] += product
            return carry

        if wide > step:
            lax.fori_loop(0, wide // step, body, 0)
        else:
            body(0, 0)

    part_rows = total // 4
    core = lax.rem(gx, 2)
    xi = gx // 2

    def part(gxi):
        return pl.ds(pl.multiple_of(gxi * part_rows, part_rows), part_rows)

    def multiply(c):
        for d in (0, 1):
            if used(d, c, hops - 1):
                ring_in(d, c, hops - 1).wait_recv()
        loads[c][0].wait()
        loads[c][1].wait()
        for t in range(count):
            add_product(t, c)
            if c == chunks - 1:
                for x in (0, 1):
                    s1[t][x] = acc[t][part(2 * x + 1 - core), :].astype(jnp.bfloat16)
                copy = send(s1[t], r1[t], s1_send.at[t], s1_recv.at[t], (sibling(gx), me))
                go(copy)
                first.append(copy)

    first = []
    groups = [range(c, min(c + GROUP, chunks)) for c in range(0, chunks, GROUP)]

    def own_sends(group):
        for c in group:
            for d in (0, 1):
                if used(d, c, 0):
                    go(ring(d, c, 0))

    own_sends(groups[0])
    for g, group in enumerate(groups):
        for s in range(1, hops):
            if s == hops - 1 and g + 1 < len(groups):
                own_sends(groups[g + 1])
            for c in group:
                for d in (0, 1):
                    ring_in(d, c, s - 1).wait_recv()
                    if used(d, c, s):
                        go(ring(d, c, s))
            if s == 1 and g > 0:
                for c in groups[g - 1]:
                    multiply(c)
    for c in groups[-1]:
        multiply(c)
    second = []
    for t in range(count):
        first[t].wait_recv()
        s2[t][...] = (
            acc[t][part(across(gx)), :] + r1[t][1 - xi].astype(jnp.float32)
        ).astype(jnp.bfloat16)
        copy = send(s2[t], r2[t], s2_send.at[t], s2_recv.at[t], (across(gx), me))
        go(copy)
        second.append(copy)
    for t in range(count):
        second[t].wait_recv()
        block = acc[t][part(gx), :] + r1[t][xi].astype(jnp.float32) + r2[t][...].astype(jnp.float32)
        for p in range(n):
            s3[t][p] = halves_stacked(block[8 * p : 8 * p + 8, :]).astype(jnp.bfloat16)
        for k in range(1, n):
            go(
                send(
                    s3[t].at[lax.rem(me + k, n)],
                    r3[t].at[me],
                    s3_send.at[t, k],
                    s3_recv.at[t, k],
                    (gx, lax.rem(me + k, n)),
                )
            )
        r3[t][me] = s3[t][me]
    for t in range(count):
        for k in range(1, n):
            owner = lax.rem(me + n - k, n)
            send(
                s3[t].at[owner], r3[t].at[owner], s3_send.at[t, k], s3_recv.at[t, k], (gx, owner)
            ).wait_recv()
        source, start, wide = tiles[t]
        out = q_out if source == 0 else kv_out
        columns = out.shape[1] // n
        half = wide // 2
        for p in range(n):
            block = r3[t][p].astype(jnp.float32)
            at = p * columns + start
            out[:, at : at + half] = block[:8].astype(jnp.bfloat16)
            out[:, at + half : at + wide] = block[8:].astype(jnp.bfloat16)
    for copy in started:
        copy.wait_send()


def project(hidden, gain, w_query, w_keyval, n):
    rows, features = hidden.shape
    width, q_cols = w_query.shape
    kv_cols = w_keyval.shape[1]
    chunks = 2
    piece = width // chunks
    total = rows * n
    step = min(1024, q_cols)
    tiles = [(0, k, step) for k in range(0, q_cols, step)] + [(1, 0, kv_cols)]
    count = len(tiles)
    hops = n // 2
    bf = jnp.bfloat16
    scratch = [
        pltpu.VMEM((chunks, piece, q_cols), bf),
        pltpu.VMEM((chunks, piece, kv_cols), bf),
        pltpu.VMEM((chunks, total, piece), bf),
    ]
    scratch += [pltpu.VMEM((total, w), jnp.float32) for _, _, w in tiles]
    for shape in (
        lambda w: (2, total // 4, w),
        lambda w: (2, total // 4, w),
        lambda w: (total // 4, w),
        lambda w: (total // 4, w),
        lambda w: (n, 16, w // 2),
        lambda w: (n, 16, w // 2),
    ):
        scratch += [pltpu.VMEM(shape(w), bf) for _, _, w in tiles]
    dma = pltpu.SemaphoreType.DMA
    scratch += [
        dma((2, chunks)),
        dma((2, chunks, hops)), dma((2, chunks, hops)),
        dma((count,)), dma((count,)),
        dma((count,)), dma((count,)),
        dma((count, n)), dma((count, n)),
    ]
    vmem = pl.BlockSpec(memory_space=pltpu.VMEM)
    hbm = pl.BlockSpec(memory_space=pl.ANY)
    return pl.pallas_call(
        functools.partial(project_kernel, n, chunks, tiles),
        out_shape=[
            jax.ShapeDtypeStruct((8, n * q_cols), bf),
            jax.ShapeDtypeStruct((8, n * kv_cols), bf),
        ],
        in_specs=[vmem, vmem, hbm, hbm],
        out_specs=[vmem, vmem],
        scratch_shapes=scratch,
        compiler_params=pltpu.CompilerParams(
            collective_id=0, has_side_effects=True, vmem_limit_bytes=VMEM_BYTES
        ),
        cost_estimate=pl.CostEstimate(
            flops=2 * total * width * (q_cols + kv_cols),
            bytes_accessed=2 * width * (q_cols + kv_cols),
            transcendentals=0,
        ),
        name="project",
    )(hidden, gain, w_query, w_keyval)


def combine_kernel(
    n, chunks,
    att_ref, w_hbm, out_ref,
    w, packed, xa, xs, part, first, ringbuf,
    w_sem, a_send, a_recv, x_send, x_recv, c_send, c_recv, e_send, e_recv, g_send, g_recv,
):
    gx = lax.axis_index("gx")
    me = lax.axis_index("gy")
    columns = w.shape[1]
    piece = w.shape[2]
    half = columns // 2
    hops = n // 2
    total = xs.shape[0]
    rows = total // n
    loads = [
        pltpu.make_async_copy(w_hbm.at[:, pl.ds(c * piece, piece)], w.at[c], w_sem.at[c])
        for c in range(chunks)
    ]
    meet(n, gx, me)
    for load in loads:
        load.start()
    for p in range(n):
        block = att_ref[:, p * columns : (p + 1) * columns].astype(jnp.float32)
        packed[p] = halves_stacked(block).astype(jnp.bfloat16)
    started = []

    def go(copy):
        copy.start()
        started.append(copy)

    met(n)
    for k in range(1, n):
        to = lax.rem(me + k, n)
        go(send(packed.at[to], xa.at[gx, me], a_send.at[k], a_recv.at[k], (gx, to)))
    xa[gx, me] = packed[me]
    other = across(gx)
    twin = sibling(gx)
    far = across(twin)
    for k in range(n):
        owner = lax.rem(me + n - k, n)
        if k:
            send(packed.at[owner], xa.at[gx, owner], a_send.at[k], a_recv.at[k], (gx, owner)).wait_recv()
        ref = xa.at[gx, owner]
        go(send(ref, ref, x_send.at[k], x_recv.at[k], (other, me)))
        go(send(ref, ref, c_send.at[k], c_recv.at[k], (twin, me)))
    for k in range(n):
        owner = lax.rem(me + n - k, n)
        ref = xa.at[other, owner]
        send(ref, ref, x_send.at[k], x_recv.at[k], (other, me)).wait_recv()
        go(send(ref, ref, e_send.at[k], e_recv.at[k], (twin, me)))
    for k in range(n):
        owner = lax.rem(me + n - k, n)
        ref = xa.at[twin, owner]
        send(ref, ref, c_send.at[k], c_recv.at[k], (twin, me)).wait_recv()
    for k in range(n):
        owner = lax.rem(me + n - k, n)
        ref = xa.at[far, owner]
        send(ref, ref, e_send.at[k], e_recv.at[k], (twin, me)).wait_recv()
    for i in range(4):
        for p in range(0, n, 2):
            low = xa[i, p].astype(jnp.float32)
            high = xa[i, p + 1].astype(jnp.float32)
            at = (i * n + p) * 8
            xs[at : at + 16, :half] = jnp.concatenate([low[:8], high[:8]], axis=0).astype(jnp.bfloat16)
            xs[at : at + 16, half:] = jnp.concatenate([low[8:], high[8:]], axis=0).astype(jnp.bfloat16)

    place = position_of(me, n)
    targets = (index_at(place + 1, n), index_at(place - 1, n))

    def used(d, c, s):
        return s > 0 or c % 2 == d

    def own(c, owner):
        return part[c, pl.ds(pl.multiple_of(owner * rows, rows), rows), :]

    def hop(d, c, s):
        begins = not (s > 0 and used(d, c, s - 1))
        src = first.at[d, c] if begins else ringbuf.at[d, c, s - 1]
        return send(src, ringbuf.at[d, c, s], g_send.at[d, c, s], g_recv.at[d, c, s], (gx, targets[d]))

    def pass_on(d, c, s):
        away = hops - s
        owner = index_at(place + away if d == 0 else place - away, n)
        value = own(c, owner)
        if s > 0 and used(d, c, s - 1):
            hop(d, c, s - 1).wait_recv()
            ringbuf[d, c, s - 1] = (
                value + ringbuf[d, c, s - 1].astype(jnp.float32)
            ).astype(jnp.bfloat16)
        else:
            first[d, c] = value.astype(jnp.bfloat16)
        go(hop(d, c, s))

    step = min(512, piece)
    for c in range(chunks):
        loads[c].wait()

        def body(k, carry):
            at = pl.multiple_of(k * step, step)
            part[c, :, pl.ds(at, step)] = jnp.dot(
                xs[...], w[c, :, pl.ds(at, step)], preferred_element_type=jnp.float32
            )
            return carry

        lax.fori_loop(0, piece // step, body, 0)
        for d in (0, 1):
            pass_on(d, c, 0 if used(d, c, 0) else 1)
    for s in range(1, hops):
        for c in range(chunks):
            for d in (0, 1):
                if s > 1 or used(d, c, 0):
                    pass_on(d, c, s)
    for c in range(chunks):
        value = own(c, me)
        for d in (0, 1):
            hop(d, c, hops - 1).wait_recv()
            value = value + ringbuf[d, c, hops - 1].astype(jnp.float32)
        out_ref[:, c * piece : (c + 1) * piece] = value.astype(jnp.bfloat16)
    for copy in started:
        copy.wait_send()


def combine(attended, w_out, n):
    columns, width = w_out.shape
    chunks = 4
    piece = width // chunks
    total = 4 * n * 8
    rows = total // n
    hops = n // 2
    bf = jnp.bfloat16
    dma = pltpu.SemaphoreType.DMA
    vmem = pl.BlockSpec(memory_space=pltpu.VMEM)
    hbm = pl.BlockSpec(memory_space=pl.ANY)
    return pl.pallas_call(
        functools.partial(combine_kernel, n, chunks),
        out_shape=jax.ShapeDtypeStruct((rows, width), bf),
        in_specs=[vmem, hbm],
        out_specs=vmem,
        scratch_shapes=[
            pltpu.VMEM((chunks, columns, piece), bf),
            pltpu.VMEM((n, 16, columns // 2), bf),
            pltpu.VMEM((4, n, 16, columns // 2), bf),
            pltpu.VMEM((total, columns), bf),
            pltpu.VMEM((chunks, total, piece), jnp.float32),
            pltpu.VMEM((2, chunks, rows, piece), bf),
            pltpu.VMEM((2, chunks, hops, rows, piece), bf),
            dma((chunks,)),
            dma((n,)), dma((n,)),
            dma((n,)), dma((n,)),
            dma((n,)), dma((n,)),
            dma((n,)), dma((n,)),
            dma((2, chunks, hops)), dma((2, chunks, hops)),
        ],
        compiler_params=pltpu.CompilerParams(
            collective_id=1, has_side_effects=True, vmem_limit_bytes=VMEM_BYTES
        ),
        cost_estimate=pl.CostEstimate(
            flops=2 * total * columns * width,
            bytes_accessed=2 * columns * width,
            transcendentals=0,
        ),
        name="combine",
    )(attended, w_out)


def shards(hidden, norm_gain, w_query, w_keyval, key_cache, value_cache, lengths, w_out):
    peers = lax.axis_size("gy")
    query, keyval = project(hidden, norm_gain, w_query, w_keyval, peers)
    attended = attend_rows(query, keyval, key_cache, value_cache, lengths)
    return combine(attended, w_out, peers)


def solution(mesh):
    in_specs = (
        P("gy", None),
        P(),
        P("gx", "gy"),
        P("gx", "gy"),
        P(("gx", "gy"), None, None, None),
        P(("gx", "gy"), None, None, None),
        P(("gx", "gy")),
        P("gy", "gx"),
    )
    out_specs = P("gy", "gx")
    return jax.shard_map(shards, mesh=mesh, in_specs=in_specs, out_specs=out_specs, check_vma=False)
```

```python
import functools
import math

import jax
import jax.numpy as jnp
from jax import lax
from jax.experimental import pallas as pl
from jax.experimental.pallas import tpu as pltpu
from jax.sharding import PartitionSpec as P

MESH = pl.DeviceIdType.MESH
VMEM_BYTES = 56 * 2**20
GROUP = 2


def rotate_heads(values, position, head_dim):
    half = head_dim // 2
    freq = jnp.exp(-(jnp.arange(half, dtype=jnp.float32) * 2.0 / head_dim) * math.log(500000.0))
    angle = position[:, None] * freq[None, :]
    cosine = jnp.cos(angle)[:, None, :]
    sine = jnp.sin(angle)[:, None, :]
    first = values[..., :half]
    second = values[..., half:]
    return jnp.concatenate(
        [first * cosine - second * sine, second * cosine + first * sine], axis=-1
    )


def attend_rows(query, keyval, key_cache, value_cache, lengths):
    rows, cache_len, kv_heads, head_dim = key_cache.shape
    heads = query.shape[1] // head_dim
    group = heads // kv_heads
    scale = 1.0 / math.sqrt(head_dim)
    position = lengths.astype(jnp.float32)
    rotated = rotate_heads(
        query.astype(jnp.float32).reshape(rows, heads, head_dim), position, head_dim
    ).astype(jnp.bfloat16)
    pairs = keyval.reshape(rows, 2, kv_heads, head_dim)
    new_key = rotate_heads(pairs[:, 0].astype(jnp.float32), position, head_dim).astype(jnp.bfloat16)
    new_value = pairs[:, 1].astype(jnp.float32)
    grouped = rotated.reshape(rows, kv_heads, group, head_dim)
    scores = (
        jnp.einsum("rgqd,rtgd->rgqt", grouped, key_cache, preferred_element_type=jnp.float32)
        * scale
    )
    own = jnp.einsum("rgqd,rgd->rgq", grouped, new_key, preferred_element_type=jnp.float32) * scale
    valid = jnp.arange(cache_len)[None, None, None, :] < lengths[:, None, None, None]
    scores = jnp.where(valid, scores, -jnp.inf)
    top = jnp.maximum(jnp.max(scores, axis=-1), own)
    weights = jnp.exp(scores - top[..., None])
    own_weight = jnp.exp(own - top)
    total = jnp.sum(weights, axis=-1) + own_weight
    probs = (weights / total[..., None]).astype(jnp.bfloat16)
    own_prob = (own_weight / total).astype(jnp.bfloat16)
    result = jnp.einsum("rgqt,rtgd->rgqd", probs, value_cache, preferred_element_type=jnp.float32)
    result = result + own_prob.astype(jnp.float32)[..., None] * new_value[:, :, None, :]
    return result.astype(jnp.bfloat16).reshape(rows, heads * head_dim)


def position_of(index, n):
    return jnp.where(lax.rem(index, 2) == 0, index // 2, n - (index + 1) // 2)


def index_at(position, n):
    position = lax.rem(position + 2 * n, n)
    return jnp.where(position < n // 2, 2 * position, 2 * n - 2 * position - 1)


def meet(n, gx, me):
    barrier = pltpu.get_barrier_semaphore()
    for k in range(1, n):
        pl.semaphore_signal(
            barrier, inc=1, device_id=(gx, lax.rem(me + k, n)), device_id_type=MESH
        )
    pl.semaphore_signal(barrier, inc=1, device_id=(sibling(gx), me), device_id_type=MESH)
    pl.semaphore_signal(barrier, inc=1, device_id=(across(gx), me), device_id_type=MESH)


def met(n):
    pl.semaphore_wait(pltpu.get_barrier_semaphore(), n + 1)


def sibling(gx):
    return gx + 1 - 2 * lax.rem(gx, 2)


def across(gx):
    return lax.rem(gx + 2, 4)


def send(src, dst, send_sem, recv_sem, device):
    copy = pltpu.make_async_remote_copy(
        src_ref=src,
        dst_ref=dst,
        send_sem=send_sem,
        recv_sem=recv_sem,
        device_id=device,
        device_id_type=MESH,
    )
    return copy


def halves_stacked(block):
    half = block.shape[1] // 2
    return jnp.concatenate([block[:, :half], block[:, half:]], axis=0)


def project_kernel(
    n, chunks, tiles,
    hidden_ref, gain_ref, wq_hbm, wkv_hbm, q_out, kv_out,
    wq, wkv, xg, *rest,
):
    count = len(tiles)
    acc = rest[:count]
    s1, r1, s2, r2, s3, r3 = (rest[count * (k + 1) : count * (k + 2)] for k in range(6))
    (w_sem, ag_send, ag_recv, s1_send, s1_recv, s2_send, s2_recv, s3_send, s3_recv) = rest[
        count * 7 :
    ]
    gx = lax.axis_index("gx")
    me = lax.axis_index("gy")
    rows = hidden_ref.shape[0]
    total = rows * n
    width = chunks * xg.shape[2]
    piece = xg.shape[2]
    hops = n // 2
    meet(n, gx, me)
    loads = []
    for c in range(chunks):
        loads.append(
            (
                pltpu.make_async_copy(
                    wq_hbm.at[pl.ds(c * piece, piece), :], wq.at[c], w_sem.at[0, c]
                ),
                pltpu.make_async_copy(
                    wkv_hbm.at[pl.ds(c * piece, piece), :], wkv.at[c], w_sem.at[1, c]
                ),
            )
        )
    for pair in loads:
        pair[0].start()
        pair[1].start()

    squares = jnp.zeros((rows, 128), jnp.float32)
    features = hidden_ref.shape[1]
    for k in range(0, features, 1024):
        block = hidden_ref[:, k : k + 1024].astype(jnp.float32)
        block = block * block
        for part in range(0, 1024, 128):
            squares = squares + block[:, part : part + 128]
    mean = jnp.sum(squares, axis=1, keepdims=True) * (1.0 / features)
    inverse = lax.rsqrt(mean + 1e-05)

    place = position_of(me, n)
    ahead = index_at(place + 1, n)
    behind = index_at(place - 1, n)
    targets = (ahead, behind)

    def slot(owner, c, d, s):
        if s < hops - 1:
            return xg.at[c, pl.ds(pl.multiple_of(owner * rows, rows), rows), :]
        half = rows // 2
        return xg.at[c, pl.ds(pl.multiple_of(owner * rows + d * half, half), half), :]

    def ring(d, c, s):
        owner = index_at(place - s if d == 0 else place + s, n)
        ref = slot(owner, c, d, s)
        return send(ref, ref, ag_send.at[d, c, s], ag_recv.at[d, c, s], (gx, targets[d]))

    def ring_in(d, c, s):
        owner = index_at(place - s - 1 if d == 0 else place + s + 1, n)
        ref = slot(owner, c, d, s)
        return send(ref, ref, ag_send.at[d, c, s], ag_recv.at[d, c, s], (gx, targets[d]))

    for c in range(chunks):
        offset = pl.multiple_of(gx * width + c * piece, piece)
        block = hidden_ref[:, pl.ds(offset, piece)].astype(jnp.float32)
        gain = gain_ref[pl.ds(offset, piece)].astype(jnp.float32).reshape(1, piece)
        xg[c, pl.ds(pl.multiple_of(me * rows, rows), rows), :] = (
            block * inverse * gain
        ).astype(jnp.bfloat16)
    met(n)

    started = []

    def go(copy):
        copy.start()
        started.append(copy)

    def add_product(t, c):
        source, start, wide = tiles[t]
        weights = wq if source == 0 else wkv
        step = min(512, wide)

        def body(k, carry):
            at = pl.multiple_of(k * step, step) if wide > step else 0
            product = jnp.dot(
                xg[c],
                weights[c, :, pl.ds(start + at, step)],
                preferred_element_type=jnp.float32,
            )
            if c == 0:
                acc[t][:, pl.ds(at, step)] = product
            else:
                acc[t][:, pl.ds(at, step)] += product
            return carry

        if wide > step:
            lax.fori_loop(0, wide // step, body, 0)
        else:
            body(0, 0)

    part_rows = total // 4
    core = lax.rem(gx, 2)
    xi = gx // 2

    def part(gxi):
        return pl.ds(pl.multiple_of(gxi * part_rows, part_rows), part_rows)

    def multiply(c):
        for d in (0, 1):
            ring_in(d, c, hops - 1).wait_recv()
        loads[c][0].wait()
        loads[c][1].wait()
        for t in range(count):
            add_product(t, c)
            if c == chunks - 1:
                for x in (0, 1):
                    s1[t][x] = acc[t][part(2 * x + 1 - core), :].astype(jnp.bfloat16)
                copy = send(s1[t], r1[t], s1_send.at[t], s1_recv.at[t], (sibling(gx), me))
                go(copy)
                first.append(copy)

    first = []
    groups = [range(c, min(c + GROUP, chunks)) for c in range(0, chunks, GROUP)]

    def own_sends(group):
        for c in group:
            for d in (0, 1):
                go(ring(d, c, 0))

    own_sends(groups[0])
    for g, group in enumerate(groups):
        for s in range(1, hops):
            if s == hops - 1 and g + 1 < len(groups):
                own_sends(groups[g + 1])
            for c in group:
                for d in (0, 1):
                    ring_in(d, c, s - 1).wait_recv()
                    go(ring(d, c, s))
            if s == 1 and g > 0:
                for c in groups[g - 1]:
                    multiply(c)
    for c in groups[-1]:
        multiply(c)
    second = []
    for t in range(count):
        first[t].wait_recv()
        s2[t][...] = (
            acc[t][part(across(gx)), :] + r1[t][1 - xi].astype(jnp.float32)
        ).astype(jnp.bfloat16)
        copy = send(s2[t], r2[t], s2_send.at[t], s2_recv.at[t], (across(gx), me))
        go(copy)
        second.append(copy)
    for t in range(count):
        second[t].wait_recv()
        block = acc[t][part(gx), :] + r1[t][xi].astype(jnp.float32) + r2[t][...].astype(jnp.float32)
        for p in range(n):
            s3[t][p] = halves_stacked(block[8 * p : 8 * p + 8, :]).astype(jnp.bfloat16)
        for k in range(1, n):
            go(
                send(
                    s3[t].at[lax.rem(me + k, n)],
                    r3[t].at[me],
                    s3_send.at[t, k],
                    s3_recv.at[t, k],
                    (gx, lax.rem(me + k, n)),
                )
            )
        r3[t][me] = s3[t][me]
    for t in range(count):
        for k in range(1, n):
            owner = lax.rem(me + n - k, n)
            send(
                s3[t].at[owner], r3[t].at[owner], s3_send.at[t, k], s3_recv.at[t, k], (gx, owner)
            ).wait_recv()
        source, start, wide = tiles[t]
        out = q_out if source == 0 else kv_out
        columns = out.shape[1] // n
        half = wide // 2
        for p in range(n):
            block = r3[t][p].astype(jnp.float32)
            at = p * columns + start
            out[:, at : at + half] = block[:8].astype(jnp.bfloat16)
            out[:, at + half : at + wide] = block[8:].astype(jnp.bfloat16)
    for copy in started:
        copy.wait_send()


def project(hidden, gain, w_query, w_keyval, n):
    rows, features = hidden.shape
    width, q_cols = w_query.shape
    kv_cols = w_keyval.shape[1]
    chunks = 2
    piece = width // chunks
    total = rows * n
    step = min(512, q_cols)
    tiles = [(0, k, step) for k in range(0, q_cols, step)] + [(1, 0, kv_cols)]
    count = len(tiles)
    hops = n // 2
    bf = jnp.bfloat16
    scratch = [
        pltpu.VMEM((chunks, piece, q_cols), bf),
        pltpu.VMEM((chunks, piece, kv_cols), bf),
        pltpu.VMEM((chunks, total, piece), bf),
    ]
    scratch += [pltpu.VMEM((total, w), jnp.float32) for _, _, w in tiles]
    for shape in (
        lambda w: (2, total // 4, w),
        lambda w: (2, total // 4, w),
        lambda w: (total // 4, w),
        lambda w: (total // 4, w),
        lambda w: (n, 16, w // 2),
        lambda w: (n, 16, w // 2),
    ):
        scratch += [pltpu.VMEM(shape(w), bf) for _, _, w in tiles]
    dma = pltpu.SemaphoreType.DMA
    scratch += [
        dma((2, chunks)),
        dma((2, chunks, hops)), dma((2, chunks, hops)),
        dma((count,)), dma((count,)),
        dma((count,)), dma((count,)),
        dma((count, n)), dma((count, n)),
    ]
    vmem = pl.BlockSpec(memory_space=pltpu.VMEM)
    hbm = pl.BlockSpec(memory_space=pl.ANY)
    return pl.pallas_call(
        functools.partial(project_kernel, n, chunks, tiles),
        out_shape=[
            jax.ShapeDtypeStruct((8, n * q_cols), bf),
            jax.ShapeDtypeStruct((8, n * kv_cols), bf),
        ],
        in_specs=[vmem, vmem, hbm, hbm],
        out_specs=[vmem, vmem],
        scratch_shapes=scratch,
        compiler_params=pltpu.CompilerParams(
            collective_id=0, has_side_effects=True, vmem_limit_bytes=VMEM_BYTES
        ),
        cost_estimate=pl.CostEstimate(
            flops=2 * total * width * (q_cols + kv_cols),
            bytes_accessed=2 * width * (q_cols + kv_cols),
            transcendentals=0,
        ),
        name="project",
    )(hidden, gain, w_query, w_keyval)


def combine_kernel(
    n, chunks,
    att_ref, w_hbm, out_ref,
    w, packed, xa, xs, part, first, ringbuf,
    w_sem, a_send, a_recv, x_send, x_recv, c_send, c_recv, e_send, e_recv, g_send, g_recv,
):
    gx = lax.axis_index("gx")
    me = lax.axis_index("gy")
    columns = w.shape[1]
    piece = w.shape[2]
    half = columns // 2
    hops = n // 2
    total = xs.shape[0]
    rows = total // n
    loads = [
        pltpu.make_async_copy(w_hbm.at[:, pl.ds(c * piece, piece)], w.at[c], w_sem.at[c])
        for c in range(chunks)
    ]
    meet(n, gx, me)
    for load in loads:
        load.start()
    for p in range(n):
        block = att_ref[:, p * columns : (p + 1) * columns].astype(jnp.float32)
        packed[p] = halves_stacked(block).astype(jnp.bfloat16)
    started = []

    def go(copy):
        copy.start()
        started.append(copy)

    met(n)
    for k in range(1, n):
        to = lax.rem(me + k, n)
        go(send(packed.at[to], xa.at[gx, me], a_send.at[k], a_recv.at[k], (gx, to)))
    xa[gx, me] = packed[me]
    other = across(gx)
    twin = sibling(gx)
    far = across(twin)
    for k in range(n):
        owner = lax.rem(me + n - k, n)
        if k:
            send(packed.at[owner], xa.at[gx, owner], a_send.at[k], a_recv.at[k], (gx, owner)).wait_recv()
        ref = xa.at[gx, owner]
        go(send(ref, ref, x_send.at[k], x_recv.at[k], (other, me)))
        go(send(ref, ref, c_send.at[k], c_recv.at[k], (twin, me)))
    for k in range(n):
        owner = lax.rem(me + n - k, n)
        ref = xa.at[other, owner]
        send(ref, ref, x_send.at[k], x_recv.at[k], (other, me)).wait_recv()
        go(send(ref, ref, e_send.at[k], e_recv.at[k], (twin, me)))
    for k in range(n):
        owner = lax.rem(me + n - k, n)
        ref = xa.at[twin, owner]
        send(ref, ref, c_send.at[k], c_recv.at[k], (twin, me)).wait_recv()
    for k in range(n):
        owner = lax.rem(me + n - k, n)
        ref = xa.at[far, owner]
        send(ref, ref, e_send.at[k], e_recv.at[k], (twin, me)).wait_recv()
    for i in range(4):
        for p in range(0, n, 2):
            low = xa[i, p].astype(jnp.float32)
            high = xa[i, p + 1].astype(jnp.float32)
            at = (i * n + p) * 8
            xs[at : at + 16, :half] = jnp.concatenate([low[:8], high[:8]], axis=0).astype(jnp.bfloat16)
            xs[at : at + 16, half:] = jnp.concatenate([low[8:], high[8:]], axis=0).astype(jnp.bfloat16)

    place = position_of(me, n)
    targets = (index_at(place + 1, n), index_at(place - 1, n))

    def used(d, c, s):
        return s > 0 or c % 2 == d

    def own(c, owner):
        return part[c, pl.ds(pl.multiple_of(owner * rows, rows), rows), :]

    def hop(d, c, s):
        begins = not (s > 0 and used(d, c, s - 1))
        src = first.at[d, c] if begins else ringbuf.at[d, c, s - 1]
        return send(src, ringbuf.at[d, c, s], g_send.at[d, c, s], g_recv.at[d, c, s], (gx, targets[d]))

    def pass_on(d, c, s):
        away = hops - s
        owner = index_at(place + away if d == 0 else place - away, n)
        value = own(c, owner)
        if s > 0 and used(d, c, s - 1):
            hop(d, c, s - 1).wait_recv()
            ringbuf[d, c, s - 1] = (
                value + ringbuf[d, c, s - 1].astype(jnp.float32)
            ).astype(jnp.bfloat16)
        else:
            first[d, c] = value.astype(jnp.bfloat16)
        go(hop(d, c, s))

    step = min(512, piece)
    for c in range(chunks):
        loads[c].wait()

        def body(k, carry):
            at = pl.multiple_of(k * step, step)
            part[c, :, pl.ds(at, step)] = jnp.dot(
                xs[...], w[c, :, pl.ds(at, step)], preferred_element_type=jnp.float32
            )
            return carry

        lax.fori_loop(0, piece // step, body, 0)
        for d in (0, 1):
            pass_on(d, c, 0 if used(d, c, 0) else 1)
    for s in range(1, hops):
        for c in range(chunks):
            for d in (0, 1):
                if s > 1 or used(d, c, 0):
                    pass_on(d, c, s)
    for c in range(chunks):
        value = own(c, me)
        for d in (0, 1):
            hop(d, c, hops - 1).wait_recv()
            value = value + ringbuf[d, c, hops - 1].astype(jnp.float32)
        out_ref[:, c * piece : (c + 1) * piece] = value.astype(jnp.bfloat16)
    for copy in started:
        copy.wait_send()


def combine(attended, w_out, n):
    columns, width = w_out.shape
    chunks = 4
    piece = width // chunks
    total = 4 * n * 8
    rows = total // n
    hops = n // 2
    bf = jnp.bfloat16
    dma = pltpu.SemaphoreType.DMA
    vmem = pl.BlockSpec(memory_space=pltpu.VMEM)
    hbm = pl.BlockSpec(memory_space=pl.ANY)
    return pl.pallas_call(
        functools.partial(combine_kernel, n, chunks),
        out_shape=jax.ShapeDtypeStruct((rows, width), bf),
        in_specs=[vmem, hbm],
        out_specs=vmem,
        scratch_shapes=[
            pltpu.VMEM((chunks, columns, piece), bf),
            pltpu.VMEM((n, 16, columns // 2), bf),
            pltpu.VMEM((4, n, 16, columns // 2), bf),
            pltpu.VMEM((total, columns), bf),
            pltpu.VMEM((chunks, total, piece), jnp.float32),
            pltpu.VMEM((2, chunks, rows, piece), bf),
            pltpu.VMEM((2, chunks, hops, rows, piece), bf),
            dma((chunks,)),
            dma((n,)), dma((n,)),
            dma((n,)), dma((n,)),
            dma((n,)), dma((n,)),
            dma((n,)), dma((n,)),
            dma((2, chunks, hops)), dma((2, chunks, hops)),
        ],
        compiler_params=pltpu.CompilerParams(
            collective_id=1, has_side_effects=True, vmem_limit_bytes=VMEM_BYTES
        ),
        cost_estimate=pl.CostEstimate(
            flops=2 * total * columns * width,
            bytes_accessed=2 * columns * width,
            transcendentals=0,
        ),
        name="combine",
    )(attended, w_out)


def shards(hidden, norm_gain, w_query, w_keyval, key_cache, value_cache, lengths, w_out):
    peers = lax.axis_size("gy")
    query, keyval = project(hidden, norm_gain, w_query, w_keyval, peers)
    attended = attend_rows(query, keyval, key_cache, value_cache, lengths)
    return combine(attended, w_out, peers)


def solution(mesh):
    in_specs = (
        P("gy", None),
        P(),
        P("gx", "gy"),
        P("gx", "gy"),
        P(("gx", "gy"), None, None, None),
        P(("gx", "gy"), None, None, None),
        P(("gx", "gy")),
        P("gy", "gx"),
    )
    out_specs = P("gy", "gx")
    return jax.shard_map(shards, mesh=mesh, in_specs=in_specs, out_specs=out_specs, check_vma=False)
```
